256 devices in a mesh: gx: 16 (over z_hi, y, core), gy: 16 (over z_lo, x).
Axes of the slice: x: 4, y: 4, z: 8 (z_hi: 2, z_lo: 4; z = z_hi * 4 + z_lo), core: 2. Of those that a mesh axis runs over, the one named last changes fastest.
Arguments:
- panel: float32 [64, 524288], P(None, ('gx', 'gy')), may hold values from -1 to 1
- trailing: float32 [524288, 512], P(('gx', 'gy')), may hold values from -6 to 6
Outputs:
- r_factor: float32 [64, 64], replicated
- projection: float32 [64, 512], replicated
- updated: float32 [524288, 512], P(('gx', 'gy'))
The draws below stay inside these ranges and needn't reach their ends.
All inputs are finite; a program needn't handle non-finite values.
Results may differ from the reference program's by a relative error of at most 0.0003.
Values sent between devices are 32-bit elements; how exact they have to be, the bound alone decides.
No kernel may reach another device: no remote copies, remote signals or barrier semaphores. Data moves between devices by JAX's collectives and lax.ppermute only.
A program may use at most 64 MiB of HBM per device.

```python
import math
import jax
import jax.numpy as jnp
from jax import lax

PANEL = 64
TRAIL = 512
ROWS = 524288


def draw_panel(key, part):
    key = jax.random.fold_in(key, 7)
    keys = jax.random.split(key, 4)
    where = jnp.arange(ROWS, dtype=jnp.float32) / ROWS
    rise = jnp.exp(where * math.log(3.0))
    rough = jnp.exp(jax.random.uniform(keys[1], (ROWS,), jnp.float32, -math.log(2.0), math.log(2.0)))
    base = jnp.clip(jax.random.normal(keys[0], (PANEL, ROWS), jnp.float32), -5.0, 5.0)
    weight = 0.6
    common = jnp.clip(jax.random.normal(keys[2], (2, ROWS), jnp.float32), -5.0, 5.0)
    coupling = jax.random.uniform(keys[3], (2, PANEL), jnp.float32, 0.3, 1.0)
    mixed = base + weight * (coupling[0][:, None] * common[0][None, :] + coupling[1][:, None] * common[1][None, :])
    values = mixed * (rise * rough)[None, :] / math.sqrt(ROWS)
    return jnp.clip(values, -1.0, 1.0)


def steps_of(rng, dims, shards, low, top_value):
    def one(position, parts):
        heights = jax.random.uniform(jax.random.fold_in(jax.random.fold_in(rng, 6), position), (parts,), jnp.float32, low / len(shards), top_value / len(shards))
        return jnp.repeat(jnp.exp(heights), dims[position] // parts).reshape((-1,) + (1,) * (len(dims) - position - 1))

    loudness = one(*shards[0])
    for cut in shards[1:]:
        loudness = loudness * one(*cut)
    return loudness


def scatter_about(own_key, dims, scale, bound, pieces=(), kind=jnp.bfloat16):
    array = jax.random.normal(own_key, dims, jnp.float32) * scale
    if len(pieces) > 0:
        array = steps_of(own_key, dims, pieces, -0.22, 0.18) * array
    return jnp.clip(array, min=-bound, max=bound).astype(kind)


def setup_inputs(seed: int = 0) -> dict:
    splits = jax.random.split(jax.random.key(seed), 3)
    panel = draw_panel(jax.random.fold_in(splits[2], 71), 0)
    trailing = scatter_about(splits[1], (ROWS, TRAIL), 1.0, 6.0, ((0, 256),), jnp.float32)
    return {"panel": panel, "trailing": trailing}


def reference(panel, trailing):
    upper = jnp.linalg.qr(panel.T, mode='r')
    signs = jnp.where(jnp.diagonal(upper) < 0, -1.0, 1.0).astype(upper.dtype)
    r_factor = signs[:, None] * upper
    basis = lax.linalg.triangular_solve(r_factor, panel, left_side=True, lower=False, transpose_a=True)
    projection = jnp.dot(basis, trailing, precision=lax.Precision.HIGHEST)
    removed = lax.dot_general(basis, projection, (((0,), (0,)), ((), ())), precision=lax.Precision.HIGHEST)
    return (r_factor, projection, trailing - removed)
```

```python
import jax
import jax.numpy as jnp
import numpy as np
from jax import lax
from jax.experimental import pallas as pl
from jax.experimental.pallas import tpu as pltpu
from jax.sharding import Mesh, PartitionSpec as P

AXES = ("zh", "y", "core", "zl", "x")
HIGH = lax.Precision.HIGHEST


def split2(value):
    hi = value.astype(jnp.bfloat16)
    lo = (value - hi.astype(jnp.float32)).astype(jnp.bfloat16)
    return hi, lo


def split3(value):
    hi = value.astype(jnp.bfloat16)
    rest = value - hi.astype(jnp.float32)
    mid = rest.astype(jnp.bfloat16)
    lo = (rest - mid.astype(jnp.float32)).astype(jnp.bfloat16)
    return hi, mid, lo


def xor_permute(value, axis, mask):
    return lax.ppermute(value, axis, [(i, i ^ mask) for i in range(lax.axis_size(axis))])


def products_kernel(panel_ref, trailing_ref, keep_ref, send_ref, acc_ref):
    step = pl.program_id(0)
    count = panel_ref.shape[0]
    hi, mid, lo = split3(panel_ref[...])
    stack = jnp.concatenate([hi, mid, lo], axis=0)
    gram = lax.dot_general(
        stack, stack, (((1,), (1,)), ((), ())), preferred_element_type=jnp.float32
    )

    def part(i, j):
        return gram[i * count : (i + 1) * count, j * count : (j + 1) * count]

    gram = part(0, 0) + (part(0, 1) + part(1, 0)) + (part(1, 1) + (part(0, 2) + part(2, 0)))
    t_hi, t_lo = split2(trailing_ref[...])
    pair = stack[: 2 * count]
    first = jnp.dot(pair, t_hi, preferred_element_type=jnp.float32)
    second = jnp.dot(pair, t_lo, preferred_element_type=jnp.float32)
    cross = first[:count] + ((first[count:] + second[:count]) + second[count:])

    @pl.when(step == 0)
    def _():
        acc_ref[:, :512] = cross
        acc_ref[:, 512:] = jnp.concatenate([gram, jnp.zeros_like(gram)], axis=1)

    @pl.when(step > 0)
    def _():
        acc_ref[:, :512] += cross
        acc_ref[:, 512:] += jnp.concatenate([gram, jnp.zeros_like(gram)], axis=1)

    @pl.when(step == pl.num_programs(0) - 1)
    def _():
        core = lax.axis_index("core")
        for target, half in ((keep_ref, core), (send_ref, 1 - core)):
            row = pl.multiple_of(half * 32, 32)
            for j in range(4):
                target[j, :32, :] = acc_ref[pl.ds(row, 32), 128 * j : 128 * (j + 1)]
                target[j, 32:, :] = acc_ref[pl.ds(pl.multiple_of(row + 8 * j, 8), 8), 512:]


def products(panel, trailing):
    rows = panel.shape[1]
    block = 512
    shape = jax.ShapeDtypeStruct((4, 40, 128), jnp.float32)
    out = pl.BlockSpec((4, 40, 128), lambda i: (0, 0, 0))
    return pl.pallas_call(
        products_kernel,
        grid=(rows // block,),
        in_specs=[
            pl.BlockSpec((64, block), lambda i: (0, i)),
            pl.BlockSpec((block, 512), lambda i: (i, 0)),
        ],
        out_specs=[out, out],
        out_shape=[shape, shape],
        scratch_shapes=[pltpu.VMEM((64, 640), jnp.float32)],
        compiler_params=pltpu.CompilerParams(vmem_limit_bytes=32 * 2**20),
        name="products",
    )(panel, trailing)


def spread_kernel(keep_ref, other_ref, *out_refs):
    here = lax.axis_index("x")
    for mask, out_ref in enumerate(out_refs):
        out_ref[...] = keep_ref[here ^ mask] + other_ref[here ^ mask]


def spread(keep, other):
    return pl.pallas_call(
        spread_kernel,
        out_shape=[jax.ShapeDtypeStruct((40, 128), jnp.float32)] * 4,
        name="spread",
    )(keep, other)


def quad_sum(value, axis, masks):
    a, b, c = [xor_permute(value, axis, m) for m in masks]
    return (value + a) + (b + c)


def eliminate(gram):
    count = gram.shape[0]
    rows = lax.broadcasted_iota(jnp.int32, (count, 2 * count), 0)
    cols = lax.broadcasted_iota(jnp.int32, (count, 2 * count), 1)
    state = jnp.where(cols < count, gram, (cols == rows + count).astype(jnp.float32))
    done = []
    for b in range(count // 8):
        for r in range(8):
            j = 8 * b + r
            pivot_row = state[r : r + 1]
            pivot = pivot_row[:, j : j + 1]
            scaled = pivot_row * (1.0 / pivot)
            factor = state[:, j : j + 1]
            left = rows[: state.shape[0]] > r
            state = state - jnp.where(left, factor, 0.0) * scaled
        done.append(state[:8])
        state = state[8:]
    full = jnp.concatenate(done, axis=0)
    diagonal = jnp.sum(jnp.where(cols == rows, full, 0.0), axis=1, keepdims=True)
    return full * lax.rsqrt(diagonal)


def finish_kernel(s0, s1, s2, s3, panel_ref, trailing_ref, r_ref, p_ref, out_ref, w_ref, g_ref, b_ref):
    @pl.when(pl.program_id(0) == 0)
    def _():
        here = lax.axis_index("x")
        for mask, ref in enumerate((s0, s1, s2, s3)):
            column = pl.multiple_of((here ^ mask) * 128, 128)
            for h in range(2):
                w_ref[32 * h : 32 * (h + 1), pl.ds(column, 128)] = ref[h, :32, :]
                row = pl.multiple_of(32 * h + 8 * (here ^ mask), 8)
                g_ref[pl.ds(row, 8), :] = ref[h, 32:, :]
        both = eliminate(g_ref[...])
        positions = lax.broadcasted_iota(jnp.int32, (64, 64), 0)
        columns = lax.broadcasted_iota(jnp.int32, (64, 64), 1)
        r_ref[...] = jnp.where(columns >= positions, both[:, :64], 0.0)
        inverse = both[:, 64:]
        projection = jnp.dot(inverse, w_ref[...], precision=HIGH, preferred_element_type=jnp.float32)
        p_ref[...] = projection
        basis = lax.dot_general(
            inverse, projection, (((0,), (0,)), ((), ())), precision=HIGH,
            preferred_element_type=jnp.float32,
        )
        hi, lo = split2(basis)
        b_ref[...] = jnp.concatenate([hi, hi, lo, lo], axis=0)

    hi, lo = split2(panel_ref[...])
    stack = jnp.concatenate([hi, lo, hi, lo], axis=0)
    removed = lax.dot_general(
        stack, b_ref[...], (((0,), (0,)), ((), ())), preferred_element_type=jnp.float32
    )
    out_ref[...] = trailing_ref[...] - removed


def finish(parts, panel, trailing):
    rows = panel.shape[1]
    block = 512
    part = pl.BlockSpec((2, 40, 128), lambda i: (0, 0, 0))
    return pl.pallas_call(
        finish_kernel,
        grid=(rows // block,),
        in_specs=[part] * 4
        + [
            pl.BlockSpec((64, block), lambda i: (0, i)),
            pl.BlockSpec((block, 512), lambda i: (i, 0)),
        ],
        out_specs=[
            pl.BlockSpec((64, 64), lambda i: (0, 0)),
            pl.BlockSpec((64, 512), lambda i: (0, 0)),
            pl.BlockSpec((block, 512), lambda i: (i, 0)),
        ],
        out_shape=[
            jax.ShapeDtypeStruct((64, 64), jnp.float32),
            jax.ShapeDtypeStruct((64, 512), jnp.float32),
            jax.ShapeDtypeStruct((rows, 512), jnp.float32),
        ],
        scratch_shapes=[
            pltpu.VMEM((64, 512), jnp.float32),
            pltpu.VMEM((64, 128), jnp.float32),
            pltpu.VMEM((256, 512), jnp.bfloat16),
        ],
        compiler_params=pltpu.CompilerParams(vmem_limit_bytes=32 * 2**20),
        name="finish",
    )(*parts, panel, trailing)


def body(panel, trailing):
    keep, send = products(panel, trailing)
    pieces = spread(keep, xor_permute(send, "core", 1))
    moved = [xor_permute(pieces[m], "x", m) for m in (1, 2, 3)]
    total = (pieces[0] + moved[0]) + (moved[1] + moved[2])
    total = quad_sum(total, "y", (1, 2, 3))
    total = quad_sum(total, ("zh", "zl"), (1, 2, 3))
    total = total + xor_permute(total, ("zh", "zl"), 6)
    other = xor_permute(total, "core", 1)
    first = lax.axis_index("core") == 0
    both = jnp.stack([jnp.where(first, total, other), jnp.where(first, other, total)])
    parts = [both] + [xor_permute(both, "x", m) for m in (1, 2, 3)]
    return tuple(finish(parts, panel, trailing))


def solution(mesh):
    fine = Mesh(mesh.devices.reshape(2, 4, 2, 4, 4), AXES)
    return jax.shard_map(
        body,
        mesh=fine,
        in_specs=(P(None, AXES), P(AXES, None)),
        out_specs=(P(), P(), P(AXES, None)),
        check_vma=False,
    )
```

```python
import jax
import jax.numpy as jnp
import numpy as np
from jax import lax
from jax.experimental import pallas as pl
from jax.experimental.pallas import tpu as pltpu
from jax.sharding import Mesh, PartitionSpec as P

AXES = ("zh", "y", "core", "zl", "x")
PRODUCTS_BLOCK = 1024
HIGH = lax.Precision.HIGHEST
PRODUCTS_VMEM = 16 * 2**20
FINISH_VMEM = 24 * 2**20


def split2(value):
    hi = value.astype(jnp.bfloat16)
    lo = (value - hi.astype(jnp.float32)).astype(jnp.bfloat16)
    return hi, lo


def split3(value):
    hi = value.astype(jnp.bfloat16)
    rest = value - hi.astype(jnp.float32)
    mid = rest.astype(jnp.bfloat16)
    lo = (rest - mid.astype(jnp.float32)).astype(jnp.bfloat16)
    return hi, mid, lo


def xor_permute(value, axis, mask):
    return lax.ppermute(value, axis, [(i, i ^ mask) for i in range(lax.axis_size(axis))])


def products_kernel(panel_hbm, trailing_hbm, out_ref, trailing_ref, panel_ref, acc_ref, panel_sem, trailing_sems):
    count = panel_ref.shape[0]
    block = PRODUCTS_BLOCK
    chunks = trailing_ref.shape[0] // block
    panel_copy = pltpu.make_async_copy(panel_hbm, panel_ref, panel_sem)
    panel_copy.start()
    copies = [
        pltpu.make_async_copy(
            trailing_hbm.at[pl.ds(i * block, block)],
            trailing_ref.at[pl.ds(i * block, block)],
            trailing_sems.at[i],
        )
        for i in range(chunks)
    ]
    for copy in copies:
        copy.start()
    panel_copy.wait()
    hi, mid, lo = split3(panel_ref[...])
    stack = jnp.concatenate([hi, mid, lo], axis=0)
    gram = lax.dot_general(
        stack, stack, (((1,), (1,)), ((), ())), preferred_element_type=jnp.float32
    )

    def part(i, j):
        return gram[i * count : (i + 1) * count, j * count : (j + 1) * count]

    gram = part(0, 0) + (part(0, 1) + part(1, 0)) + (part(1, 1) + (part(0, 2) + part(2, 0)))
    acc_ref[:, 512:] = jnp.concatenate([gram, jnp.zeros_like(gram)], axis=1)
    total = None
    for i in range(chunks):
        copies[i].wait()
        t_hi, t_lo = split2(trailing_ref[i * block : (i + 1) * block])
        pair = stack[: 2 * count, i * block : (i + 1) * block]
        first = jnp.dot(pair, t_hi, preferred_element_type=jnp.float32)
        second = jnp.dot(pair, t_lo, preferred_element_type=jnp.float32)
        cross = first[:count] + ((first[count:] + second[:count]) + second[count:])
        total = cross if total is None else total + cross
    acc_ref[:, :512] = total
    for half in range(2):
        for j in range(4):
            row = 32 * half + 8 * j
            out_ref[4 * half + j, :32, :] = acc_ref[32 * half : 32 * half + 32, 128 * j : 128 * (j + 1)]
            out_ref[4 * half + j, 32:, :] = acc_ref[row : row + 8, 512:]


def products(panel, trailing):
    rows = panel.shape[1]
    block = PRODUCTS_BLOCK
    return pl.pallas_call(
        products_kernel,
        in_specs=[pl.BlockSpec(memory_space=pl.ANY)] * 2,
        out_specs=[pl.BlockSpec(memory_space=pltpu.VMEM)] * 2,
        out_shape=[
            jax.ShapeDtypeStruct((8, 40, 128), jnp.float32),
            pltpu.VMEM((rows, 512), jnp.float32),
        ],
        scratch_shapes=[
            pltpu.VMEM((64, rows), jnp.float32),
            pltpu.VMEM((64, 640), jnp.float32),
            pltpu.SemaphoreType.DMA,
            pltpu.SemaphoreType.DMA((rows // block,)),
        ],
        compiler_params=pltpu.CompilerParams(vmem_limit_bytes=PRODUCTS_VMEM),
        name="products",
    )(*[pltpu.with_memory_space_constraint(a, pltpu.HBM) for a in (panel, trailing)])


def small_call(kernel, count, shape, name):
    return pl.pallas_call(
        kernel,
        in_specs=[pl.BlockSpec(memory_space=pltpu.VMEM)] * count,
        out_specs=pl.BlockSpec(memory_space=pltpu.VMEM),
        out_shape=jax.ShapeDtypeStruct(shape, jnp.float32),
        compiler_params=pltpu.CompilerParams(vmem_limit_bytes=4 * 2**20),
        name=name,
    )


def add_up_kernel(parts_ref, out_ref):
    total = [parts_ref[i] for i in range(parts_ref.shape[0])]
    while len(total) > 1:
        total = [a + b for a, b in zip(total[::2], total[1::2])]
    out_ref[...] = total[0]


def pair_kernel(mine_ref, other_ref, out_ref):
    core = lax.axis_index("core")
    out_ref[core] = mine_ref[...]
    out_ref[1 - core] = other_ref[...]


def quad_sum(value, axis, masks):
    a, b, c = [xor_permute(value, axis, m) for m in masks]
    return (value + a) + (b + c)


def eliminate(gram):
    count = gram.shape[0]
    wide = 2 * count
    rows = lax.broadcasted_iota(jnp.int32, (count, wide), 0)
    cols = lax.broadcasted_iota(jnp.int32, (count, wide), 1)
    state = jnp.where(cols < count, gram, (cols == rows + count).astype(jnp.float32))
    blocks = [state[8 * b : 8 * b + 8] for b in range(count // 8)]

    def spread_lane(value, j):
        return jnp.broadcast_to(value[:, j : j + 1], (value.shape[0], wide))

    done = []
    for b in range(count // 8):
        j0 = 8 * b
        row = [blocks[b][i : i + 1] for i in range(8)]
        pivots = [[spread_lane(row[k], j0 + i) for k in range(i + 1)] for i in range(8)]
        columns = {
            c: [spread_lane(blocks[c], j0 + k) for k in range(8)]
            for c in range(b + 1, count // 8)
        }
        inverse, lower = [], {}
        for k in range(8):
            inverse.append(1.0 / pivots[k][k])
            for i in range(k + 1, 8):
                lower[i, k] = pivots[i][k] * inverse[k]
            for i in range(k + 1, 8):
                for m in range(k + 1, i + 1):
                    pivots[i][m] = pivots[i][m] - lower[i, k] * pivots[m][k]
        for i in range(8):
            for k in range(i):
                row[i] = row[i] - lower[i, k] * row[k]
        solved = [row[i] * inverse[i] for i in range(8)]
        for i in reversed(range(8)):
            for k in range(i + 1, 8):
                solved[i] = solved[i] - lower[k, i] * solved[k]
        for c in range(b + 1, count // 8):
            taken = columns[c][0] * solved[0]
            for k in range(1, 8):
                taken = taken + columns[c][k] * solved[k]
            blocks[c] = blocks[c] - taken
        done += row
    full = jnp.concatenate(done, axis=0)
    diagonal = jnp.sum(jnp.where(cols == rows, full, 0.0), axis=1, keepdims=True)
    return full * lax.rsqrt(diagonal)


def finish_kernel(
    s0, s1, s2, s3, panel_ref, trailing_ref, r_ref, p_ref, out_hbm,
    w_ref, g_ref, out_ref, out_sems,
):
    chunks, block, _ = out_ref.shape
    stores = [
        pltpu.make_async_copy(
            out_ref.at[i], out_hbm.at[pl.ds(i * block, block)], out_sems.at[i]
        )
        for i in range(chunks)
    ]
    here = lax.axis_index("x")
    for mask, ref in enumerate((s0, s1, s2, s3)):
        column = pl.multiple_of((here ^ mask) * 128, 128)
        for h in range(2):
            w_ref[32 * h : 32 * (h + 1), pl.ds(column, 128)] = ref[h, :32, :]
            row = pl.multiple_of(32 * h + 8 * (here ^ mask), 8)
            g_ref[pl.ds(row, 8), :] = ref[h, 32:, :]
    both = eliminate(g_ref[...])
    positions = lax.broadcasted_iota(jnp.int32, (64, 64), 0)
    columns = lax.broadcasted_iota(jnp.int32, (64, 64), 1)
    r_ref[...] = jnp.where(columns >= positions, both[:, :64], 0.0)
    inverse = both[:, 64:]
    projection = jnp.dot(inverse, w_ref[...], precision=HIGH, preferred_element_type=jnp.float32)
    p_ref[...] = projection
    basis = lax.dot_general(
        inverse, projection, (((0,), (0,)), ((), ())), precision=HIGH,
        preferred_element_type=jnp.float32,
    )
    hi, lo = split2(basis)
    right = jnp.concatenate([hi, hi, lo, lo], axis=0)
    for i in range(chunks):
        hi, lo = split2(panel_ref[:, i * block : (i + 1) * block])
        left = jnp.concatenate([hi, lo], axis=0).T
        left = jnp.concatenate([left, left], axis=1)
        removed = jnp.dot(left, right, preferred_element_type=jnp.float32)
        out_ref[i] = trailing_ref[i * block : (i + 1) * block] - removed
        stores[i].start()
    for store in stores:
        store.wait()


def finish(parts, panel, trailing):
    rows = panel.shape[1]
    block = 512
    vmem = pl.BlockSpec(memory_space=pltpu.VMEM)
    far = pl.BlockSpec(memory_space=pl.ANY)
    return pl.pallas_call(
        finish_kernel,
        in_specs=[vmem] * 6,
        out_specs=[vmem, vmem, far],
        out_shape=[
            jax.ShapeDtypeStruct((64, 64), jnp.float32),
            jax.ShapeDtypeStruct((64, 512), jnp.float32),
            jax.ShapeDtypeStruct((rows, 512), jnp.float32),
        ],
        scratch_shapes=[
            pltpu.VMEM((64, 512), jnp.float32),
            pltpu.VMEM((64, 128), jnp.float32),
            pltpu.VMEM((rows // block, block, 512), jnp.float32),
            pltpu.SemaphoreType.DMA((rows // block,)),
        ],
        compiler_params=pltpu.CompilerParams(vmem_limit_bytes=FINISH_VMEM),
        name="finish",
    )(*parts, panel, pltpu.with_memory_space_constraint(trailing, pltpu.VMEM))


def all_send(value, axes):
    return lax.all_to_all(value, axes, 0, 0, tiled=True)


def body(panel, trailing):
    sums, trailing = products(panel, trailing)
    total = small_call(add_up_kernel, 1, (40, 128), "add_up")(all_send(sums, ("core", "x")))
    total = quad_sum(total, "y", (1, 2, 3))
    total = quad_sum(total, ("zh", "zl"), (1, 2, 3))
    total = total + xor_permute(total, ("zh", "zl"), 6)
    other = xor_permute(total, "core", 1)
    both = small_call(pair_kernel, 2, (2, 40, 128), "pair")(total, other)
    parts = [both] + [xor_permute(both, "x", m) for m in (1, 2, 3)]
    return tuple(finish(parts, panel, trailing))


def solution(mesh):
    fine = Mesh(mesh.devices.reshape(2, 4, 2, 4, 4), AXES)
    return jax.shard_map(
        body,
        mesh=fine,
        in_specs=(P(None, AXES), P(AXES, None)),
        out_specs=(P(), P(), P(AXES, None)),
        check_vma=False,
    )
```

```python
import jax
import jax.numpy as jnp
import numpy as np
from jax import lax
from jax.experimental import pallas as pl
from jax.experimental.pallas import tpu as pltpu
from jax.sharding import Mesh, PartitionSpec as P

AXES = ("zh", "y", "core", "zl", "x")
PRODUCTS_BLOCK = 1024
HIGH = lax.Precision.HIGHEST
PRODUCTS_VMEM = 16 * 2**20
FINISH_VMEM = 24 * 2**20


def split2(value):
    hi = value.astype(jnp.bfloat16)
    lo = (value - hi.astype(jnp.float32)).astype(jnp.bfloat16)
    return hi, lo


def split3(value):
    hi = value.astype(jnp.bfloat16)
    rest = value - hi.astype(jnp.float32)
    mid = rest.astype(jnp.bfloat16)
    lo = (rest - mid.astype(jnp.float32)).astype(jnp.bfloat16)
    return hi, mid, lo


def xor_permute(value, axis, mask):
    return lax.ppermute(value, axis, [(i, i ^ mask) for i in range(lax.axis_size(axis))])


def products_kernel(panel_hbm, trailing_hbm, out_ref, trailing_ref, panel_ref, acc_ref, panel_sem, trailing_sems):
    count = panel_ref.shape[0]
    block = PRODUCTS_BLOCK
    chunks = trailing_ref.shape[0] // block
    panel_copy = pltpu.make_async_copy(panel_hbm, panel_ref, panel_sem)
    panel_copy.start()
    copies = [
        pltpu.make_async_copy(
            trailing_hbm.at[pl.ds(i * block, block)],
            trailing_ref.at[pl.ds(i * block, block)],
            trailing_sems.at[i],
        )
        for i in range(chunks)
    ]
    for copy in copies:
        copy.start()
    panel_copy.wait()
    hi, mid, lo = split3(panel_ref[...])
    stack = jnp.concatenate([hi, mid, lo], axis=0)
    nt = (((1,), (1,)), ((), ()))
    outer = lax.dot_general(stack, hi, nt, preferred_element_type=jnp.float32)
    middle = lax.dot_general(mid, mid, nt, preferred_element_type=jnp.float32)
    side = outer[count : 2 * count] + outer[2 * count :]
    gram = outer[:count] + ((side + side.T) + middle)
    acc_ref[:, 512:] = jnp.concatenate([gram, jnp.zeros_like(gram)], axis=1)
    total = None
    for i in range(chunks):
        copies[i].wait()
        t_hi, t_lo = split2(trailing_ref[i * block : (i + 1) * block])
        pair = stack[: 2 * count, i * block : (i + 1) * block]
        first = jnp.dot(pair, t_hi, preferred_element_type=jnp.float32)
        second = jnp.dot(pair, t_lo, preferred_element_type=jnp.float32)
        cross = first[:count] + ((first[count:] + second[:count]) + second[count:])
        total = cross if total is None else total + cross
    acc_ref[:, :512] = total
    for half in range(2):
        for j in range(4):
            row = 32 * half + 8 * j
            out_ref[4 * half + j, :32, :] = acc_ref[32 * half : 32 * half + 32, 128 * j : 128 * (j + 1)]
            out_ref[4 * half + j, 32:, :] = acc_ref[row : row + 8, 512:]


def products(panel, trailing):
    rows = panel.shape[1]
    block = PRODUCTS_BLOCK
    return pl.pallas_call(
        products_kernel,
        in_specs=[pl.BlockSpec(memory_space=pl.ANY)] * 2,
        out_specs=[pl.BlockSpec(memory_space=pltpu.VMEM)] * 2,
        out_shape=[
            jax.ShapeDtypeStruct((8, 40, 128), jnp.float32),
            pltpu.VMEM((rows, 512), jnp.float32),
        ],
        scratch_shapes=[
            pltpu.VMEM((64, rows), jnp.float32),
            pltpu.VMEM((64, 640), jnp.float32),
            pltpu.SemaphoreType.DMA,
            pltpu.SemaphoreType.DMA((rows // block,)),
        ],
        compiler_params=pltpu.CompilerParams(vmem_limit_bytes=PRODUCTS_VMEM),
        name="products",
    )(*[pltpu.with_memory_space_constraint(a, pltpu.HBM) for a in (panel, trailing)])


def small_call(kernel, count, shape, name):
    return pl.pallas_call(
        kernel,
        in_specs=[pl.BlockSpec(memory_space=pltpu.VMEM)] * count,
        out_specs=pl.BlockSpec(memory_space=pltpu.VMEM),
        out_shape=jax.ShapeDtypeStruct(shape, jnp.float32),
        compiler_params=pltpu.CompilerParams(vmem_limit_bytes=4 * 2**20),
        name=name,
    )


def add_up_kernel(parts_ref, out_ref):
    total = [parts_ref[i] for i in range(parts_ref.shape[0])]
    while len(total) > 1:
        total = [a + b for a, b in zip(total[::2], total[1::2])]
    out_ref[...] = total[0]


def pair_kernel(mine_ref, other_ref, out_ref):
    core = lax.axis_index("core")
    out_ref[core] = mine_ref[...]
    out_ref[1 - core] = other_ref[...]


def quad_sum(value, axis, masks):
    a, b, c = [xor_permute(value, axis, m) for m in masks]
    return (value + a) + (b + c)


def eliminate(gram):
    count = gram.shape[0]
    wide = 2 * count
    rows = lax.broadcasted_iota(jnp.int32, (count, wide), 0)
    cols = lax.broadcasted_iota(jnp.int32, (count, wide), 1)
    state = jnp.where(cols < count, gram, (cols == rows + count).astype(jnp.float32))
    blocks = [state[8 * b : 8 * b + 8] for b in range(count // 8)]

    def spread_lane(value, j):
        return jnp.broadcast_to(value[:, j : j + 1], (value.shape[0], wide))

    done = []
    for b in range(count // 8):
        j0 = 8 * b
        row = [blocks[b][i : i + 1] for i in range(8)]
        pivots = [[spread_lane(row[k], j0 + i) for k in range(i + 1)] for i in range(8)]
        columns = {
            c: [spread_lane(blocks[c], j0 + k) for k in range(8)]
            for c in range(b + 1, count // 8)
        }
        inverse, lower = [], {}
        for k in range(8):
            inverse.append(1.0 / pivots[k][k])
            for i in range(k + 1, 8):
                lower[i, k] = pivots[i][k] * inverse[k]
            for i in range(k + 1, 8):
                for m in range(k + 1, i + 1):
                    pivots[i][m] = pivots[i][m] - lower[i, k] * pivots[m][k]
        for i in range(8):
            for k in range(i):
                row[i] = row[i] - lower[i, k] * row[k]
        solved = [row[i] * inverse[i] for i in range(8)]
        for i in reversed(range(8)):
            for k in range(i + 1, 8):
                solved[i] = solved[i] - lower[k, i] * solved[k]
        for c in range(b + 1, count // 8):
            taken = columns[c][0] * solved[0]
            for k in range(1, 8):
                taken = taken + columns[c][k] * solved[k]
            blocks[c] = blocks[c] - taken
        done += row
    full = jnp.concatenate(done, axis=0)
    diagonal = jnp.sum(jnp.where(cols == rows, full, 0.0), axis=1, keepdims=True)
    return full * lax.rsqrt(diagonal)


def finish_kernel(
    s0, s1, s2, s3, panel_ref, trailing_ref, r_ref, p_ref, out_hbm,
    w_ref, g_ref, out_ref, out_sems,
):
    chunks, block, _ = out_ref.shape
    stores = [
        pltpu.make_async_copy(
            out_ref.at[i], out_hbm.at[pl.ds(i * block, block)], out_sems.at[i]
        )
        for i in range(chunks)
    ]
    here = lax.axis_index("x")
    for mask, ref in enumerate((s0, s1, s2, s3)):
        column = pl.multiple_of((here ^ mask) * 128, 128)
        for h in range(2):
            w_ref[32 * h : 32 * (h + 1), pl.ds(column, 128)] = ref[h, :32, :]
            row = pl.multiple_of(32 * h + 8 * (here ^ mask), 8)
            g_ref[pl.ds(row, 8), :] = ref[h, 32:, :]
    both = eliminate(g_ref[...])
    positions = lax.broadcasted_iota(jnp.int32, (64, 64), 0)
    columns = lax.broadcasted_iota(jnp.int32, (64, 64), 1)
    r_ref[...] = jnp.where(columns >= positions, both[:, :64], 0.0)
    inverse = both[:, 64:]
    projection = jnp.dot(inverse, w_ref[...], precision=HIGH, preferred_element_type=jnp.float32)
    p_ref[...] = projection
    basis = lax.dot_general(
        inverse, projection, (((0,), (0,)), ((), ())), precision=HIGH,
        preferred_element_type=jnp.float32,
    )
    hi, lo = split2(basis)
    right = jnp.concatenate([hi, hi, lo, lo], axis=0)
    for i in range(chunks):
        hi, lo = split2(panel_ref[:, i * block : (i + 1) * block])
        left = jnp.concatenate([hi, lo], axis=0).T
        left = jnp.concatenate([left, left], axis=1)
        removed = jnp.dot(left, right, preferred_element_type=jnp.float32)
        out_ref[i] = trailing_ref[i * block : (i + 1) * block] - removed
        stores[i].start()
    for store in stores:
        store.wait()


def finish(parts, panel, trailing):
    rows = panel.shape[1]
    block = 512
    vmem = pl.BlockSpec(memory_space=pltpu.VMEM)
    far = pl.BlockSpec(memory_space=pl.ANY)
    return pl.pallas_call(
        finish_kernel,
        in_specs=[vmem] * 6,
        out_specs=[vmem, vmem, far],
        out_shape=[
            jax.ShapeDtypeStruct((64, 64), jnp.float32),
            jax.ShapeDtypeStruct((64, 512), jnp.float32),
            jax.ShapeDtypeStruct((rows, 512), jnp.float32),
        ],
        scratch_shapes=[
            pltpu.VMEM((64, 512), jnp.float32),
            pltpu.VMEM((64, 128), jnp.float32),
            pltpu.VMEM((rows // block, block, 512), jnp.float32),
            pltpu.SemaphoreType.DMA((rows // block,)),
        ],
        compiler_params=pltpu.CompilerParams(vmem_limit_bytes=FINISH_VMEM),
        name="finish",
    )(*parts, panel, pltpu.with_memory_space_constraint(trailing, pltpu.VMEM))


def all_send(value, axes):
    return lax.all_to_all(value, axes, 0, 0, tiled=True)


def body(panel, trailing):
    sums, trailing = products(panel, trailing)
    total = small_call(add_up_kernel, 1, (40, 128), "add_up")(all_send(sums, ("core", "x")))
    total = quad_sum(total, "y", (1, 2, 3))
    total = quad_sum(total, ("zh", "zl"), (1, 2, 3))
    total = total + xor_permute(total, ("zh", "zl"), 7)
    other = xor_permute(total, "core", 1)
    both = small_call(pair_kernel, 2, (2, 40, 128), "pair")(total, other)
    parts = [both] + [xor_permute(both, "x", m) for m in (1, 2, 3)]
    return tuple(finish(parts, panel, trailing))


def solution(mesh):
    fine = Mesh(mesh.devices.reshape(2, 4, 2, 4, 4), AXES)
    return jax.shard_map(
        body,
        mesh=fine,
        in_specs=(P(None, AXES), P(AXES, None)),
        out_specs=(P(), P(), P(AXES, None)),
        check_vma=False,
    )
```

```python
import jax
import jax.numpy as jnp
import numpy as np
from jax import lax
from jax.experimental import pallas as pl
from jax.experimental.pallas import tpu as pltpu
from jax.sharding import Mesh, PartitionSpec as P

AXES = ("zh", "y", "core", "zl", "x")
PRODUCTS_BLOCK = 1024
HIGH = lax.Precision.HIGHEST
PRODUCTS_VMEM = 16 * 2**20
FINISH_VMEM = 24 * 2**20


def split2(value):
    hi = value.astype(jnp.bfloat16)
    lo = (value - hi.astype(jnp.float32)).astype(jnp.bfloat16)
    return hi, lo


def split3(value):
    hi = value.astype(jnp.bfloat16)
    rest = value - hi.astype(jnp.float32)
    mid = rest.astype(jnp.bfloat16)
    lo = (rest - mid.astype(jnp.float32)).astype(jnp.bfloat16)
    return hi, mid, lo


def xor_permute(value, axis, mask):
    return lax.ppermute(value, axis, [(i, i ^ mask) for i in range(lax.axis_size(axis))])


def products_kernel(panel_hbm, trailing_hbm, out_ref, trailing_ref, panel_ref, acc_ref, panel_sem, trailing_sems):
    count = panel_ref.shape[0]
    block = PRODUCTS_BLOCK
    chunks = trailing_ref.shape[0] // block
    panel_copy = pltpu.make_async_copy(panel_hbm, panel_ref, panel_sem)
    panel_copy.start()
    copies = [
        pltpu.make_async_copy(
            trailing_hbm.at[pl.ds(i * block, block)],
            trailing_ref.at[pl.ds(i * block, block)],
            trailing_sems.at[i],
        )
        for i in range(chunks)
    ]
    for i, copy in enumerate(copies):
        copy.start(priority=i % 2)
    panel_copy.wait()
    hi, mid, lo = split3(panel_ref[...])
    stack = jnp.concatenate([hi, mid, lo], axis=0)
    nt = (((1,), (1,)), ((), ()))
    outer = lax.dot_general(stack, hi, nt, preferred_element_type=jnp.float32)
    middle = lax.dot_general(mid, mid, nt, preferred_element_type=jnp.float32)
    side = outer[count : 2 * count] + outer[2 * count :]
    gram = outer[:count] + ((side + side.T) + middle)
    acc_ref[:, 512:] = jnp.concatenate([gram, jnp.zeros_like(gram)], axis=1)
    total = None
    for i in range(chunks):
        copies[i].wait()
        t_hi, t_lo = split2(trailing_ref[i * block : (i + 1) * block])
        pair = stack[: 2 * count, i * block : (i + 1) * block]
        first = jnp.dot(pair, t_hi, preferred_element_type=jnp.float32)
        second = jnp.dot(pair, t_lo, preferred_element_type=jnp.float32)
        cross = first[:count] + ((first[count:] + second[:count]) + second[count:])
        total = cross if total is None else total + cross
    acc_ref[:, :512] = total
    for half in range(2):
        for j in range(4):
            row = 32 * half + 8 * j
            out_ref[4 * half + j, :32, :] = acc_ref[32 * half : 32 * half + 32, 128 * j : 128 * (j + 1)]
            out_ref[4 * half + j, 32:, :] = acc_ref[row : row + 8, 512:]


def products(panel, trailing):
    rows = panel.shape[1]
    block = PRODUCTS_BLOCK
    return pl.pallas_call(
        products_kernel,
        in_specs=[pl.BlockSpec(memory_space=pl.ANY)] * 2,
        out_specs=[pl.BlockSpec(memory_space=pltpu.VMEM)] * 2,
        out_shape=[
            jax.ShapeDtypeStruct((8, 40, 128), jnp.float32),
            pltpu.VMEM((rows, 512), jnp.float32),
        ],
        scratch_shapes=[
            pltpu.VMEM((64, rows), jnp.float32),
            pltpu.VMEM((64, 640), jnp.float32),
            pltpu.SemaphoreType.DMA,
            pltpu.SemaphoreType.DMA((rows // block,)),
        ],
        compiler_params=pltpu.CompilerParams(vmem_limit_bytes=PRODUCTS_VMEM),
        name="products",
    )(*[pltpu.with_memory_space_constraint(a, pltpu.HBM) for a in (panel, trailing)])


def small_call(kernel, count, shape, name):
    return pl.pallas_call(
        kernel,
        in_specs=[pl.BlockSpec(memory_space=pltpu.VMEM)] * count,
        out_specs=pl.BlockSpec(memory_space=pltpu.VMEM),
        out_shape=jax.ShapeDtypeStruct(shape, jnp.float32),
        compiler_params=pltpu.CompilerParams(vmem_limit_bytes=4 * 2**20),
        name=name,
    )


def add_up_kernel(parts_ref, out_ref):
    total = [parts_ref[i] for i in range(parts_ref.shape[0])]
    while len(total) > 1:
        total = [a + b for a, b in zip(total[::2], total[1::2])]
    out_ref[...] = total[0]


def pair_kernel(mine_ref, other_ref, out_ref):
    core = lax.axis_index("core")
    out_ref[core] = mine_ref[...]
    out_ref[1 - core] = other_ref[...]


def quad_sum(value, axis, masks):
    a, b, c = [xor_permute(value, axis, m) for m in masks]
    return (value + a) + (b + c)


def eliminate(gram):
    count = gram.shape[0]
    wide = 2 * count
    rows = lax.broadcasted_iota(jnp.int32, (count, wide), 0)
    cols = lax.broadcasted_iota(jnp.int32, (count, wide), 1)
    state = jnp.where(cols < count, gram, (cols == rows + count).astype(jnp.float32))
    blocks = [state[8 * b : 8 * b + 8] for b in range(count // 8)]

    def spread_lane(value, j):
        return jnp.broadcast_to(value[:, j : j + 1], (value.shape[0], wide))

    done = []
    for b in range(count // 8):
        j0 = 8 * b
        row = [blocks[b][i : i + 1] for i in range(8)]
        pivots = [[spread_lane(row[k], j0 + i) for k in range(i + 1)] for i in range(8)]
        columns = {
            c: [spread_lane(blocks[c], j0 + k) for k in range(8)]
            for c in range(b + 1, count // 8)
        }
        inverse, lower = [], {}
        for k in range(8):
            inverse.append(1.0 / pivots[k][k])
            for i in range(k + 1, 8):
                lower[i, k] = pivots[i][k] * inverse[k]
            for i in range(k + 1, 8):
                for m in range(k + 1, i + 1):
                    pivots[i][m] = pivots[i][m] - lower[i, k] * pivots[m][k]
        for i in range(8):
            for k in range(i):
                row[i] = row[i] - lower[i, k] * row[k]
        solved = [row[i] * inverse[i] for i in range(8)]
        for i in reversed(range(8)):
            for k in range(i + 1, 8):
                solved[i] = solved[i] - lower[k, i] * solved[k]
        for c in range(b + 1, count // 8):
            taken = columns[c][0] * solved[0]
            for k in range(1, 8):
                taken = taken + columns[c][k] * solved[k]
            blocks[c] = blocks[c] - taken
        done += row
    full = jnp.concatenate(done, axis=0)
    diagonal = jnp.sum(jnp.where(cols == rows, full, 0.0), axis=1, keepdims=True)
    return full * lax.rsqrt(diagonal)


def finish_kernel(
    s0, s1, s2, s3, panel_ref, trailing_ref, r_ref, p_ref, out_hbm,
    w_ref, g_ref, out_ref, out_sems,
):
    chunks, block, _ = out_ref.shape
    stores = [
        pltpu.make_async_copy(
            out_ref.at[i], out_hbm.at[pl.ds(i * block, block)], out_sems.at[i]
        )
        for i in range(chunks)
    ]
    here = lax.axis_index("x")
    for mask, ref in enumerate((s0, s1, s2, s3)):
        column = pl.multiple_of((here ^ mask) * 128, 128)
        for h in range(2):
            w_ref[32 * h : 32 * (h + 1), pl.ds(column, 128)] = ref[h, :32, :]
            row = pl.multiple_of(32 * h + 8 * (here ^ mask), 8)
            g_ref[pl.ds(row, 8), :] = ref[h, 32:, :]
    both = eliminate(g_ref[...])
    positions = lax.broadcasted_iota(jnp.int32, (64, 64), 0)
    columns = lax.broadcasted_iota(jnp.int32, (64, 64), 1)
    r_ref[...] = jnp.where(columns >= positions, both[:, :64], 0.0)
    inverse = both[:, 64:]
    projection = jnp.dot(inverse, w_ref[...], precision=HIGH, preferred_element_type=jnp.float32)
    p_ref[...] = projection
    basis = lax.dot_general(
        inverse, projection, (((0,), (0,)), ((), ())), precision=HIGH,
        preferred_element_type=jnp.float32,
    )
    hi, lo = split2(basis)
    right = jnp.concatenate([hi, hi, lo, lo], axis=0)
    for i in range(chunks):
        hi, lo = split2(panel_ref[:, i * block : (i + 1) * block])
        left = jnp.concatenate([hi, lo], axis=0).T
        left = jnp.concatenate([left, left], axis=1)
        removed = jnp.dot(left, right, preferred_element_type=jnp.float32)
        out_ref[i] = trailing_ref[i * block : (i + 1) * block] - removed
        stores[i].start(priority=i % 2)
    for store in stores:
        store.wait()


def finish(parts, panel, trailing):
    rows = panel.shape[1]
    block = 512
    vmem = pl.BlockSpec(memory_space=pltpu.VMEM)
    far = pl.BlockSpec(memory_space=pl.ANY)
    return pl.pallas_call(
        finish_kernel,
        in_specs=[vmem] * 6,
        out_specs=[vmem, vmem, far],
        out_shape=[
            jax.ShapeDtypeStruct((64, 64), jnp.float32),
            jax.ShapeDtypeStruct((64, 512), jnp.float32),
            jax.ShapeDtypeStruct((rows, 512), jnp.float32),
        ],
        scratch_shapes=[
            pltpu.VMEM((64, 512), jnp.float32),
            pltpu.VMEM((64, 128), jnp.float32),
            pltpu.VMEM((rows // block, block, 512), jnp.float32),
            pltpu.SemaphoreType.DMA((rows // block,)),
        ],
        compiler_params=pltpu.CompilerParams(vmem_limit_bytes=FINISH_VMEM),
        name="finish",
    )(*parts, panel, pltpu.with_memory_space_constraint(trailing, pltpu.VMEM))


def all_send(value, axes):
    return lax.all_to_all(value, axes, 0, 0, tiled=True)


def body(panel, trailing):
    sums, trailing = products(panel, trailing)
    total = small_call(add_up_kernel, 1, (40, 128), "add_up")(all_send(sums, ("core", "x")))
    total = quad_sum(total, "y", (1, 2, 3))
    total = quad_sum(total, ("zh", "zl"), (1, 2, 3))
    total = total + xor_permute(total, ("zh", "zl"), 7)
    other = xor_permute(total, "core", 1)
    both = small_call(pair_kernel, 2, (2, 40, 128), "pair")(total, other)
    parts = [both] + [xor_permute(both, "x", m) for m in (1, 2, 3)]
    return tuple(finish(parts, panel, trailing))


def solution(mesh):
    fine = Mesh(mesh.devices.reshape(2, 4, 2, 4, 4), AXES)
    return jax.shard_map(
        body,
        mesh=fine,
        in_specs=(P(None, AXES), P(AXES, None)),
        out_specs=(P(), P(), P(AXES, None)),
        check_vma=False,
    )
```
